256 devices in a mesh: shot: 8 (over z), trace: 32 (over y, x, core).
Axes of the slice: x: 4, y: 4, z: 8, core: 2. Of those that a mesh axis runs over, the one named last changes fastest.
Arguments:
- gathers: bfloat16 [16, 2048, 4096], P('shot', 'trace'), may hold values from -6 to 6
- first_strided_weight: bfloat16 [4, 128], replicated, may hold values from -3 to 3
- second_strided_weight: bfloat16 [512, 128], replicated, may hold values from -0.25 to 0.25
- second_dilated_weight: bfloat16 [384, 128], replicated, may hold values from -0.3125 to 0.3125
- second_pointwise_weight: bfloat16 [128, 128], replicated, may hold values from -0.5 to 0.5
- third_strided_weight: bfloat16 [512, 128], replicated, may hold values from -0.25 to 0.25
- third_dilated_weight: bfloat16 [384, 128], replicated, may hold values from -0.3125 to 0.3125
- third_pointwise_weight: bfloat16 [128, 128], replicated, may hold values from -0.5 to 0.5
- final_strided_weight: bfloat16 [512, 128], replicated, may hold values from -0.25 to 0.25
- codebooks: bfloat16 [8, 1024, 128], replicated, may hold values from -3 to 3
- codes: int32 [16, 4096, 8, 8], P('shot', 'trace'), may hold values from 0 to 1023
- dest: int32 [8, 32, 256, 1], P('shot', 'trace'), may hold values from 0 to 255; in each aligned block of 256 rows (0 to 255, 256 to 511, ..., all dimensions but the last counted through in order) at most 2 rows name the same one
- bins: int32 [8, 32, 256], P('shot', 'trace'), may hold values from 0 to 63
Outputs:
- stack_code: float32 [16384, 8, 128], P(('shot', 'trace'))
- stack_resid: float32 [16384, 8, 128], P(('shot', 'trace'))
The draws below stay inside these ranges and needn't reach their ends.
Inputs may be any that keep to these rules, and one draw needn't show every extreme that they name: `dest`: among one device's 256 rows at most 2 name the same owner, a bound that some block reaches of them.
All inputs are finite; a program needn't handle non-finite values.
Results may differ from the reference program's by a relative error of at most 0.0085.
Values may be sent and summed in bfloat16 or wider, within the bound.
A program may use at most 128 MiB of HBM per device.

```python
import math
import jax
import jax.numpy as jnp
import numpy as np
from jax import lax

ENCODER_CHANNELS = 128
K = 1024
NQ = 8
SH_GRP = 2
TR_DEV = 128
NS = 2048
BINS_DEV = 64
SHOTS = 16
TRACES = 4096
ROWS_DEV = 256
FR = 8
CAP = 2
N_SHOT = 8
N_TRACE = 32
DEVICES = 256


def touch_ends(array, stream_key, least, high):
    extent = array.shape
    place = [jax.random.randint(jax.random.fold_in(stream_key, axis), (), 0, extent[axis]) for axis in range(len(extent))]
    array = array.at[tuple(place)].set(least)
    longest = extent.index(max(extent))
    place[longest] = (place[longest] + 1) % extent[longest]
    return array.at[tuple(place)].set(high)


def shard_levels(own_key, shape, pieces, smallest, largest):
    gain = 1.0
    for axis_at, parts in pieces:
        heights = jax.random.uniform(jax.random.fold_in(jax.random.fold_in(own_key, 6), axis_at), (parts,), jnp.float32, smallest / len(pieces), largest / len(pieces))
        gain = gain * jnp.repeat(jnp.exp(heights), shape[axis_at] // parts).reshape((-1,) + (1,) * (len(shape) - 1 - axis_at))
    return gain


def assign_block(stream_key, own, number, rows, number_of, top, limit, skew):
    order = jax.random.permutation(stream_key, number_of)
    heavy_load, common = load_shares(number_of, rows * top, limit, skew, True), load_shares(number_of, rows * top, limit, skew, False)
    places = jnp.arange(number_of)

    def named(sizes, rotation):
        used = int((sizes > 0).sum())
        fixed = max(1, used // 4)
        passed = fixed + (places - fixed + rotation * (used - fixed)) % max(1, number_of - fixed)
        return jnp.zeros((number_of,), jnp.int32).at[order[jnp.where(places < fixed, places, passed)]].set(jnp.asarray(sizes, jnp.int32))

    sizes = jnp.where(number % 4 == 0, named(heavy_load, number // 4), named(common, number - number // 4 - 1))
    mixed = jax.random.permutation(jax.random.fold_in(own, 3), number_of)
    source_of, receiver = mixed[0:number_of // 2 * 2:2], mixed[1:number_of // 2 * 2:2]
    slack = jnp.minimum(sizes[source_of] - 1, limit - sizes[receiver]) // 2
    slack = jnp.where((source_of == order[0]) | (receiver == order[0]) | (sizes[receiver] == 0), 0, jnp.maximum(slack, 0))
    passed = jax.random.randint(jax.random.fold_in(own, 4), (number_of // 2,), 0, 1 << 20) % (slack + 1)
    sizes = sizes.at[source_of].add(-passed).at[receiver].add(passed)
    members = jnp.searchsorted(jnp.cumsum(sizes), jnp.arange(rows * top), side="right").astype(jnp.int32)
    grid = members.reshape(top, rows).T
    grid = grid[jax.random.permutation(jax.random.fold_in(own, 1), rows)]
    rotation = jax.random.randint(jax.random.fold_in(own, 2), (rows, 1), 0, top)
    return jnp.take_along_axis(grid, (jnp.arange(top)[None, :] + rotation) % top, axis=1)


def load_shares(count, total, reach, slope, full):
    weights = [(1 << 20) // math.isqrt(rank ** slope) + 1 for rank in range(1, count + 1)]
    largest = reach if full else min(reach, max(-(-total // count), total * weights[0] // sum(weights)))
    least = 1 if total - largest >= count - 1 else 0
    holding, rest = [largest] + [least] * (count - 1), total - largest - least * (count - 1)
    while rest > 0:
        candidates = [i for i in range(1, count) if holding[i] < largest] or [i for i in range(1, count) if holding[i] < reach]
        mass, budget = sum([weights[i] for i in candidates]), rest
        for i in candidates:
            addition = min(reach - holding[i], max(1, budget * weights[i] // mass), rest)
            holding[i] = holding[i] + addition
            rest = rest - addition
    return np.array(holding)


def normal_values(stream_key, dims, deviation, bound, shards=(), kind=jnp.bfloat16):
    array = jax.random.normal(stream_key, dims, jnp.float32) * deviation
    if len(shards) > 0:
        array = shard_levels(stream_key, dims, shards, -0.22, 0.18) * array
    return jnp.clip(array, min=-bound, max=bound).astype(kind)


def setup_inputs(seed: int = 0) -> dict:
    streams_of = jax.random.split(jax.random.key(seed), 14)
    gathers = normal_values(streams_of[0], (SHOTS, NS, TRACES), 1.0, 6.0, ((0, 8), (1, 32)))
    first_strided_weight = normal_values(streams_of[1], (4, ENCODER_CHANNELS), 4 ** -0.5, 3.0)
    second_strided_weight = normal_values(streams_of[2], (4 * ENCODER_CHANNELS, ENCODER_CHANNELS), (4 * ENCODER_CHANNELS) ** -0.5, 0.25)
    second_dilated_weight = normal_values(streams_of[3], (3 * ENCODER_CHANNELS, ENCODER_CHANNELS), (3 * ENCODER_CHANNELS) ** -0.5, 0.3125)
    second_pointwise_weight = normal_values(streams_of[4], (ENCODER_CHANNELS, ENCODER_CHANNELS), ENCODER_CHANNELS ** -0.5, 0.5)
    third_strided_weight = normal_values(streams_of[5], (4 * ENCODER_CHANNELS, ENCODER_CHANNELS), (4 * ENCODER_CHANNELS) ** -0.5, 0.25)
    third_dilated_weight = normal_values(streams_of[6], (3 * ENCODER_CHANNELS, ENCODER_CHANNELS), (3 * ENCODER_CHANNELS) ** -0.5, 0.3125)
    third_pointwise_weight = normal_values(streams_of[7], (ENCODER_CHANNELS, ENCODER_CHANNELS), ENCODER_CHANNELS ** -0.5, 0.5)
    final_strided_weight = normal_values(streams_of[8], (4 * ENCODER_CHANNELS, ENCODER_CHANNELS), (4 * ENCODER_CHANNELS) ** -0.5, 0.25)
    codebooks = normal_values(streams_of[9], (NQ, K, ENCODER_CHANNELS), 0.5, 3.0)
    codes = touch_ends(jax.random.randint(streams_of[10], (SHOTS, TRACES, FR, NQ), 0, K), jax.random.fold_in(streams_of[10], 1), 0, K - 1).astype(jnp.int32)
    dest_keys = jax.random.split(jax.random.fold_in(streams_of[11], 1), N_SHOT * N_TRACE * ROWS_DEV // ROWS_DEV)
    dest_turns = jax.random.permutation(jax.random.fold_in(streams_of[11], 3), N_SHOT * N_TRACE * ROWS_DEV // ROWS_DEV)
    dest = jax.vmap(lambda own, number: assign_block(jax.random.fold_in(streams_of[11], 2), own, number, ROWS_DEV, DEVICES, 1, CAP, 2))(dest_keys, dest_turns).reshape((N_SHOT, N_TRACE, ROWS_DEV, 1))
    bins = touch_ends(jax.random.randint(streams_of[12], (N_SHOT, N_TRACE, ROWS_DEV), 0, BINS_DEV), jax.random.fold_in(streams_of[12], 1), 0, BINS_DEV - 1).astype(jnp.int32)
    return dict(gathers=gathers, first_strided_weight=first_strided_weight, second_strided_weight=second_strided_weight, second_dilated_weight=second_dilated_weight, second_pointwise_weight=second_pointwise_weight, third_strided_weight=third_strided_weight, third_dilated_weight=third_dilated_weight, third_pointwise_weight=third_pointwise_weight, final_strided_weight=final_strided_weight, codebooks=codebooks, codes=codes, dest=dest, bins=bins)


def matrix_product(value_entries, weight):
    leading = value_entries.shape[:-1]
    flat_rows = value_entries.reshape(-1, value_entries.shape[-1])
    result = jnp.dot(flat_rows, weight, preferred_element_type=jnp.float32)
    return result.reshape(leading + (weight.shape[1],))


def strided(value_entries, weight):
    batch, length, channels = value_entries.shape
    return matrix_product(value_entries.reshape(batch, length // 4, 4 * channels), weight)


def residual_unit_block(value_entries, dilated_weight, pointwise_weight, dilation_factor):
    length = value_entries.shape[1]
    activated = jax.nn.elu(value_entries.astype(jnp.float32)).astype(jnp.bfloat16)
    padded = jnp.pad(activated, ((0, 0), (dilation_factor, dilation_factor), (0, 0)))
    kernel_tap_rows = jnp.concatenate([padded[:, :length], activated, padded[:, 2 * dilation_factor:]], axis=2)
    inner_total_sum = matrix_product(kernel_tap_rows, dilated_weight)
    middle = jax.nn.elu(inner_total_sum).astype(jnp.bfloat16)
    outer_sum = matrix_product(middle, pointwise_weight)
    return (value_entries.astype(jnp.float32) + outer_sum).astype(jnp.bfloat16)


def encode_block(signal, weight_tensors):
    first_strided_weight, second_strided_weight, second_dilated_weight, second_pointwise_weight, third_strided_weight, third_dilated_weight, third_pointwise_weight, final_strided_weight = weight_tensors
    samples, width_block = signal.shape
    regrouped = signal.reshape(samples // 4, 4, width_block).transpose(2, 0, 1)
    first = matrix_product(regrouped, first_strided_weight)
    first = jax.nn.elu(first).astype(jnp.bfloat16)
    second_result = jax.nn.elu(strided(first, second_strided_weight)).astype(jnp.bfloat16)
    second_result = residual_unit_block(second_result, second_dilated_weight, second_pointwise_weight, 3)
    third_block_part = jax.nn.elu(strided(second_result, third_strided_weight)).astype(jnp.bfloat16)
    third_block_part = residual_unit_block(third_block_part, third_dilated_weight, third_pointwise_weight, 3)
    return strided(third_block_part, final_strided_weight)


def encode(signal, weight_tensors):
    count_items, samples, traces = signal.shape
    block_width = math.gcd(traces, 32)
    block_count = traces // block_width
    blocks = signal.reshape(count_items, samples, block_count, block_width).transpose(0, 2, 1, 3)
    blocks = blocks.reshape(count_items * block_count, samples, block_width)
    encoded = lax.map(lambda block_in: encode_block(block_in, weight_tensors), blocks)
    return encoded.reshape(count_items, traces, encoded.shape[2], encoded.shape[3])


def decode(code_ids, codebooks):
    summed = jnp.zeros(code_ids.shape[:-1] + (codebooks.shape[2],), jnp.float32)
    for section in range(codebooks.shape[0]):
        summed = summed + jnp.take(codebooks[section], code_ids[..., section], axis=0).astype(jnp.float32)
    return summed


def device_rows(value_entries):
    frames, channels = value_entries.shape[2], value_entries.shape[3]
    shaped = value_entries.reshape(N_SHOT, SH_GRP, N_TRACE, TR_DEV, frames, channels).transpose(0, 2, 1, 3, 4, 5)
    return shaped.reshape(N_SHOT * N_TRACE * SH_GRP * TR_DEV, frames * channels)


def reference(gathers, first_strided_weight, second_strided_weight, second_dilated_weight, second_pointwise_weight, third_strided_weight, third_dilated_weight, third_pointwise_weight, final_strided_weight, codebooks, codes, dest, bins):
    weight_tensors = (first_strided_weight, second_strided_weight, second_dilated_weight, second_pointwise_weight, third_strided_weight, third_dilated_weight, third_pointwise_weight, final_strided_weight)
    latent = encode(gathers, weight_tensors)
    decoded = decode(codes, codebooks)
    residue = latent - decoded
    frames, channels = latent.shape[2], latent.shape[3]
    total_bins = N_SHOT * N_TRACE * BINS_DEV
    keys = (dest.reshape(-1).astype(jnp.int32) * BINS_DEV + bins.reshape(-1).astype(jnp.int32)).astype(jnp.int32)
    ones = jnp.ones(keys.shape, jnp.float32)
    fold_count = jnp.maximum(jax.ops.segment_sum(ones, keys, total_bins), jnp.float32(1.0))
    stack_code = jax.ops.segment_sum(device_rows(decoded), keys, total_bins) / fold_count[:, None]
    stack_resid = jax.ops.segment_sum(device_rows(residue), keys, total_bins) / fold_count[:, None]
    return (stack_code.reshape(total_bins, frames, channels), stack_resid.reshape(total_bins, frames, channels))
```

```python
import jax
import jax.numpy as jnp
from jax import lax
from jax.experimental import pallas as pl
from jax.experimental.pallas import tpu as pltpu
from jax.sharding import PartitionSpec as P

F32, BF16, I32 = jnp.float32, jnp.bfloat16, jnp.int32
MESH = pl.DeviceIdType.MESH
NZ, NP = 8, 32
ROWS, HALF, FR, C = 256, 128, 8, 128
NB = 4
GROUPS = NP // NB
BINS = 64
SLOTS = 2 * NZ * NP


def elu(x):
    low = jnp.exp(x) - 1.0
    return jnp.maximum(x.astype(BF16), jnp.minimum(low.astype(BF16), 0.0))


def dot(a, b):
    return jnp.dot(a, b, preferred_element_type=F32)


def dot_nt(a, b):
    return lax.dot_general(a, b, (((1,), (1,)), ((), ())), preferred_element_type=F32)


def iota(shape, axis):
    return lax.broadcasted_iota(I32, shape, axis)


def hot(mask):
    return jnp.where(mask, 1.0, 0.0).astype(BF16)


def lanes(parts):
    return jnp.concatenate(parts, axis=1)


def bytes_of(ref, sem):
    return pltpu.make_async_copy(ref, ref, sem)


def residual(skip, act, wd, wp, rows, stack):
    def body(step, carry):
        bases = [6 * (step * stack + n) for n in range(stack)]
        taps = jnp.concatenate(
            [
                lanes(
                    [act[pl.ds(t + 3 * i, 3), rows].reshape(3 * HALF, C) for i in range(4)]
                )
                for t in bases
            ],
            axis=0,
        )
        outer = dot(elu(dot(taps, wd[...])), wp[...])
        for n, t in enumerate(bases):
            for i in range(2):
                piece = outer[n * 3 * HALF : (n + 1) * 3 * HALF, C * i : C * (i + 1)]
                at = pl.ds(t + 3 * i, 3)
                old = skip[at, rows].astype(F32)
                skip[at, rows] = (old + piece.reshape(3, HALF, C)).astype(BF16)
        return carry

    return body


def kernel(
    g, w1_in, w2_in, w2d_in, w2p_in, w3_in, w3d_in, w3p_in, w4_in, cb_in, codes_in, dest, bins,
    out_code, out_resid,
    w1, w2, w2d, w2p, w3, w3d, w3p, w4, cb, codes,
    w1_wide, w2d_pair, w2p_pair, w3d_pair, w3p_pair,
    got, s_mid, s_act, t_mid, t_act, order, place, relay, lat,
    meta_tab, meta_z, meta_mid, meta_own, tab, rows_z, rows_mid, rows_own, pick, dec,
    load_sem, own_sem, g_send, g_recv, mz_send, mz_recv, mp_send, mp_recv,
    z_send, z_recv, p_send, p_recv,
):
    z, p = lax.axis_index("shot"), lax.axis_index("trace")

    loads = [
        pltpu.make_async_copy(src, dst, load_sem.at[i])
        for i, (src, dst) in enumerate(
            [
                (codes_in, codes), (w1_in, w1), (w2_in, w2), (w2d_in, w2d), (w2p_in, w2p),
                (w3_in, w3), (w3d_in, w3d), (w3p_in, w3p), (w4_in, w4), (cb_in, cb),
            ]
        )
    ]
    for load in loads:
        load.start()
    own_block = pltpu.make_async_copy(
        g.at[:, :, pl.ds(pl.multiple_of(p * C, C), C)], got.at[p], own_sem
    )
    own_block.start()

    barrier = pltpu.get_barrier_semaphore()

    def greet_plane(j, carry):
        pl.semaphore_signal(
            barrier, inc=1, device_id={"trace": lax.rem(p + j, NP)}, device_id_type=MESH
        )
        return carry

    def greet_z(j, carry):
        pl.semaphore_signal(
            barrier, inc=1, device_id={"shot": lax.rem(z + j, NZ)}, device_id_type=MESH
        )
        return carry

    lax.fori_loop(1, NP, greet_plane, 0)
    lax.fori_loop(1, NZ, greet_z, 0)
    pl.semaphore_wait(barrier, NP - 1 + NZ - 1)

    def send_block(j, carry):
        to = lax.rem(p - j + NP, NP)
        pltpu.make_async_remote_copy(
            src_ref=g.at[:, :, pl.ds(pl.multiple_of(to * C, C), C)],
            dst_ref=got.at[p],
            send_sem=g_send,
            recv_sem=g_recv.at[j // NB],
            device_id={"trace": to},
            device_id_type=MESH,
        ).start()
        return carry

    lax.fori_loop(1, NP, send_block, 0)

    sub, lane = iota((ROWS, ROWS), 0), iota((ROWS, ROWS), 1)
    dest_row = dest[...]
    dest_f = dest_row.astype(F32)
    dest_col = jnp.sum(jnp.where(sub == lane, dest_f, 0.0), axis=1, keepdims=True)
    same = dest_col == dest_f
    rank_row = jnp.sum(jnp.where(same & (sub < lane), 1.0, 0.0), axis=0, keepdims=True)
    rank_col = jnp.sum(jnp.where(same & (lane < sub), 1.0, 0.0), axis=1, keepdims=True)
    seconds_before = jnp.sum(
        jnp.where((rank_col > 0.5) & (sub < lane), 1.0, 0.0), axis=0, keepdims=True
    )
    seconds = jnp.sum(rank_row, axis=1, keepdims=True)
    index = iota((1, ROWS), 1).astype(F32)
    position = jnp.where(rank_row > 0.5, seconds_before, seconds + index - seconds_before)
    order[...] = hot(position == sub.astype(F32))
    owner_hit = dest_row == sub
    slot_hot = [hot(owner_hit & (rank_row < 0.5)), hot(owner_hit & (rank_row > 0.5))]
    for r in range(2):
        place[r] = dot_nt(slot_hot[r], order[...]).astype(BF16)
    i, j = iota((SLOTS, SLOTS), 0), iota((SLOTS, SLOTS), 1)
    relay[...] = hot(j == (i % 16) * 32 + i // 16)

    loads[0].wait()
    low = jnp.zeros((ROWS, 64), F32)
    high = jnp.zeros((ROWS, 64), F32)
    for f in range(FR):
        ids = codes[:, :, f, :].reshape(ROWS, 8)
        spread = hot(iota((8, 64), 1) == iota((8, 64), 0) + 8 * f)
        low = low + dot((ids % 256).astype(F32).astype(BF16), spread)
        high = high + dot((ids // 256).astype(F32).astype(BF16), spread)
    bin_col = jnp.sum(
        jnp.where(sub == lane, bins[...].astype(F32) + 1.0, 0.0), axis=1, keepdims=True
    )
    bin_part = jnp.where(iota((ROWS, C), 1) == 0, bin_col, 0.0)
    meta = lanes([low.astype(BF16), high.astype(BF16), bin_part.astype(BF16)])
    for r in range(2):
        meta_tab[:, r] = dot(slot_hot[r], meta).astype(BF16).reshape(NZ, NP, 2 * C)
    meta_z[z] = meta_tab[z]

    def send_meta_z(j, carry):
        to = lax.rem(z + j, NZ)
        pltpu.make_async_remote_copy(
            src_ref=meta_tab.at[to],
            dst_ref=meta_z.at[z],
            send_sem=mz_send,
            recv_sem=mz_recv,
            device_id={"shot": to},
            device_id_type=MESH,
        ).start()
        return carry

    lax.fori_loop(1, NZ, send_meta_z, 0)

    for load in loads[1:9]:
        load.wait()
    tall = jnp.concatenate([w1[...].astype(F32)] * 16, axis=0)
    for t in range(16):
        w1_wide[:, C * t : C * (t + 1)] = jnp.where(iota((64, C), 0) // 4 == t, tall, 0.0).astype(
            BF16
        )
    zero = jnp.zeros((C, C), BF16)
    for wd, wp, wd_pair, wp_pair in ((w2d, w2p, w2d_pair, w2p_pair), (w3d, w3p, w3d_pair, w3p_pair)):
        wd_pair[0 : 3 * C, 0:C] = wd[...]
        wd_pair[3 * C : 4 * C, 0:C] = zero
        wd_pair[0:C, C : 2 * C] = zero
        wd_pair[C : 4 * C, C : 2 * C] = wd[...]
        wp_pair[0:C, 0:C] = wp[...]
        wp_pair[0:C, C : 2 * C] = zero
        wp_pair[C : 2 * C, 0:C] = zero
        wp_pair[C : 2 * C, C : 2 * C] = wp[...]
    edge = jnp.zeros((ROWS, C), BF16)
    for act, frames in ((s_act, 128), (t_act, 32)):
        for n in range(3):
            act[n] = edge
        for n in range(act.shape[0] - frames - 3):
            act[frames + 3 + n] = edge
    for mid, frames in ((s_mid, 128), (t_mid, 32)):
        for n in range(mid.shape[0] - frames):
            mid[frames + n] = edge

    def encode_group(i):
        sources = [lax.rem(p + i * NB + n, NP) for n in range(NB)]
        x = jnp.concatenate(
            [dot_nt(order[...], lanes([got[s, 0], got[s, 1]])).astype(BF16) for s in sources],
            axis=0,
        )
        for q in range(4):
            first = elu(dot(x, w1_wide[:, 4 * C * q : 4 * C * (q + 1)]))
            second = elu(dot(first, w2[...]))
            active = elu(second.astype(F32))
            for n, s in enumerate(sources):
                part = slice(n * ROWS, (n + 1) * ROWS)
                s_mid[4 * s + q] = second[part]
                s_act[4 * s + q + 3] = active[part]

    own_block.wait()
    bytes_of(got.at[pl.ds(0, NB - 1)], g_recv.at[0]).wait()

    def later_group(i, carry):
        @pl.when(i > 0)
        def _():
            bytes_of(got.at[pl.ds(0, NB)], g_recv.at[i]).wait()

        encode_group(i)
        return carry

    lax.fori_loop(0, 2, later_group, 0)

    bytes_of(meta_z.at[pl.ds(0, NZ - 1)], mz_recv).wait()
    meta_mid[...] = (
        dot(relay[...], meta_z[...].reshape(SLOTS, 2 * C)).astype(BF16).reshape(NP, 16, 2 * C)
    )
    meta_own[p] = meta_mid[p]

    def send_meta_p(j, carry):
        to = lax.rem(p + j, NP)
        pltpu.make_async_remote_copy(
            src_ref=meta_mid.at[to],
            dst_ref=meta_own.at[p],
            send_sem=mp_send,
            recv_sem=mp_recv,
            device_id={"trace": to},
            device_id_type=MESH,
        ).start()
        return carry

    lax.fori_loop(1, NP, send_meta_p, 0)
    lax.fori_loop(2, GROUPS, later_group, 0)

    def encode_half(h):
        rows = pl.ds(h * HALF, HALF)
        lax.fori_loop(0, 11, residual(s_mid, s_act, w2d_pair, w2p_pair, rows, 2), 0)

        def third(j, carry):
            taps = jnp.concatenate(
                [
                    lanes([s_mid[4 * (8 * j + n) + i, rows] for i in range(4)])
                    for n in range(8)
                ],
                axis=0,
            )
            u = elu(dot(taps, w3[...]))
            active = elu(u.astype(F32))
            t_mid[pl.ds(8 * j, 8), rows] = u.reshape(8, HALF, C)
            t_act[pl.ds(8 * j + 3, 8), rows] = active.reshape(8, HALF, C)
            return carry

        lax.fori_loop(0, 4, third, 0)
        lax.fori_loop(0, 3, residual(t_mid, t_act, w3d_pair, w3p_pair, rows, 2), 0)
        taps = jnp.concatenate(
            [lanes([t_mid[4 * n + i, rows] for i in range(4)]) for n in range(8)], axis=0
        )
        lat[:, rows] = dot(taps, w4[...]).astype(BF16).reshape(FR, HALF, C)

    def fill_table(r, count):
        wide = lanes([lat[f, 0:count] for f in range(FR)])
        table = dot(place[r, :, 0:count], wide).astype(BF16)
        for f in range(FR):
            tab[r, :, f] = table[:, C * f : C * (f + 1)].reshape(NZ, NP, C)
        rows_z[z, r] = tab[r, z]

    def send_z(r, f0, n, sem):
        def go(j, carry):
            to = lax.rem(z + j, NZ)
            pltpu.make_async_remote_copy(
                src_ref=tab.at[r, to, pl.ds(f0, n)],
                dst_ref=rows_z.at[z, r, pl.ds(f0, n)],
                send_sem=z_send.at[sem],
                recv_sem=z_recv.at[sem],
                device_id={"shot": to},
                device_id_type=MESH,
            ).start()
            return carry

        lax.fori_loop(1, NZ, go, 0)

    encode_half(0)
    fill_table(1, HALF)
    send_z(1, 0, FR, 0)
    encode_half(1)
    fill_table(0, ROWS)
    for c in range(4):
        send_z(0, 2 * c, 2, c + 1)

    bytes_of(meta_own.at[pl.ds(0, NP - 1)], mp_recv).wait()
    loads[9].wait()
    meta_rows = meta_own[...].reshape(SLOTS, 2 * C)

    def split_codes(f, carry):
        a, b = iota((2 * C, C), 0), iota((2 * C, C), 1)
        want = jnp.where(b < 8, 8 * f + b, 64 + 8 * f + b - 8)
        pick[f] = dot(meta_rows, hot((a == want) & (b < 16)))
        return carry

    lax.fori_loop(0, FR, split_codes, 0)

    def decode(f):
        total = jnp.zeros((SLOTS, C), F32)
        for k in range(8):
            low = pick[f, :, k : k + 1]
            high = pick[f, :, 8 + k : 9 + k]
            one = hot(low == iota((SLOTS, 256), 1).astype(F32))
            book = lanes([cb[k, 256 * n : 256 * (n + 1)] for n in range(4)])
            parts = dot(one, book)
            total = total + jnp.where(
                high < 1.5,
                jnp.where(high < 0.5, parts[:, 0:C], parts[:, C : 2 * C]),
                jnp.where(high < 2.5, parts[:, 2 * C : 3 * C], parts[:, 3 * C :]),
            )
        dec[f] = total

    def decode_some(f, carry):
        decode(f)
        return carry

    bytes_of(rows_z.at[pl.ds(0, NZ - 1), 1], z_recv.at[0]).wait()
    for c in range(4):
        lax.fori_loop(2 * c, 2 * c + 2, decode_some, 0)
        f0 = 2 * c
        bytes_of(rows_z.at[pl.ds(0, NZ - 1), 0, pl.ds(f0, 2)], z_recv.at[c + 1]).wait()
        both = lanes([rows_z[:, :, f0 + n].reshape(SLOTS, C) for n in range(2)])
        moved = dot(relay[...], both).astype(BF16)
        for n in range(2):
            rows_mid[:, f0 + n] = moved[:, C * n : C * (n + 1)].reshape(NP, 16, C)
        rows_own[p, f0 : f0 + 2] = rows_mid[p, f0 : f0 + 2]

        def send_p(j, carry):
            to = lax.rem(p + j, NP)
            pltpu.make_async_remote_copy(
                src_ref=rows_mid.at[to, pl.ds(f0, 2)],
                dst_ref=rows_own.at[p, pl.ds(f0, 2)],
                send_sem=p_send.at[c],
                recv_sem=p_recv.at[c],
                device_id={"trace": to},
                device_id_type=MESH,
            ).start()
            return carry

        lax.fori_loop(1, NP, send_p, 0)

    sel = hot((iota((8, 2 * C), 1) == C) & (iota((8, 2 * C), 0) == 0))
    bin_row = dot_nt(sel, meta_rows)[0:1]
    member = bin_row == (iota((BINS, SLOTS), 0) + 1).astype(F32)
    fold = jnp.maximum(jnp.sum(jnp.where(member, 1.0, 0.0), axis=1, keepdims=True), 1.0)
    member = hot(member)
    for f in range(FR):
        big = dec[f].astype(BF16)
        rest = (dec[f] - big.astype(F32)).astype(BF16)
        sums = dot(member, lanes([big, rest]))
        out_code[:, f, :] = (sums[:, 0:C] + sums[:, C : 2 * C]) / fold
    for c in range(4):
        f0 = 2 * c
        bytes_of(rows_own.at[pl.ds(0, NP - 1), pl.ds(f0, 2)], p_recv.at[c]).wait()
        both = lanes([rows_own[:, f0 + n].reshape(SLOTS, C) for n in range(2)])
        sums = dot(member, both)
        for n in range(2):
            out_resid[:, f0 + n, :] = (
                sums[:, C * n : C * (n + 1)] / fold - out_code[:, f0 + n, :]
            )

    bytes_of(got.at[pl.ds(0, NP - 1)], g_send).wait()
    bytes_of(meta_z.at[pl.ds(0, NZ - 1)], mz_send).wait()
    bytes_of(meta_own.at[pl.ds(0, NP - 1)], mp_send).wait()
    bytes_of(rows_z.at[pl.ds(0, NZ - 1), 1], z_send.at[0]).wait()
    for c in range(4):
        bytes_of(rows_z.at[pl.ds(0, NZ - 1), 0, pl.ds(2 * c, 2)], z_send.at[c + 1]).wait()
        bytes_of(rows_own.at[pl.ds(0, NP - 1), pl.ds(2 * c, 2)], p_send.at[c]).wait()


def on_device(
    gathers, w1, w2, w2d, w2p, w3, w3d, w3p, w4, codebooks, codes, dest, bins
):
    hbm, vmem = pl.BlockSpec(memory_space=pl.ANY), pl.BlockSpec(memory_space=pltpu.VMEM)
    scratch = [
        ((4, C), BF16), ((4 * C, C), BF16), ((3 * C, C), BF16), ((C, C), BF16),
        ((4 * C, C), BF16), ((3 * C, C), BF16), ((C, C), BF16), ((4 * C, C), BF16),
        ((8, 1024, C), BF16), ((2, 128, 8, 8), I32),
        ((64, 16 * C), BF16), ((4 * C, 2 * C), BF16), ((2 * C, 2 * C), BF16),
        ((4 * C, 2 * C), BF16), ((2 * C, 2 * C), BF16),
        ((NP, 2, 64, C), BF16),
        ((132, ROWS, C), BF16), ((138, ROWS, C), BF16),
        ((36, ROWS, C), BF16), ((42, ROWS, C), BF16),
        ((ROWS, ROWS), BF16), ((2, ROWS, ROWS), BF16), ((SLOTS, SLOTS), BF16),
        ((FR, ROWS, C), BF16),
        ((NZ, 2, NP, 2 * C), BF16), ((NZ, 2, NP, 2 * C), BF16),
        ((NP, 16, 2 * C), BF16), ((NP, 16, 2 * C), BF16),
        ((2, NZ, FR, NP, C), BF16), ((NZ, 2, FR, NP, C), BF16),
        ((NP, FR, 16, C), BF16), ((NP, FR, 16, C), BF16),
        ((FR, SLOTS, C), F32), ((FR, SLOTS, C), F32),
    ]
    dma = pltpu.SemaphoreType.DMA
    return pl.pallas_call(
        kernel,
        out_shape=[jax.ShapeDtypeStruct((BINS, FR, C), F32)] * 2,
        in_specs=[hbm] * 11 + [vmem] * 2,
        out_specs=[vmem] * 2,
        scratch_shapes=[pltpu.VMEM(shape, kind) for shape, kind in scratch]
        + [
            dma((10,)), dma, dma, dma((GROUPS,)), dma, dma, dma, dma,
            dma((5,)), dma((5,)), dma((4,)), dma((4,)),
        ],
        compiler_params=pltpu.CompilerParams(
            collective_id=0, has_side_effects=True, vmem_limit_bytes=60 * 2**20
        ),
        name="codec_stack",
    )(
        gathers, w1, w2, w2d, w2p, w3, w3d, w3p, w4, codebooks, codes,
        dest.reshape(1, ROWS), bins.reshape(1, ROWS),
    )


def solution(mesh):
    rows4, rows3 = P("shot", "trace", None, None), P("shot", "trace", None)
    out = P(("shot", "trace"), None, None)
    return jax.shard_map(
        on_device,
        mesh=mesh,
        in_specs=(rows3,) + (P(),) * 9 + (rows4, rows4, rows3),
        out_specs=(out, out),
        check_vma=False,
    )
```

```python
import jax
import jax.numpy as jnp
from jax import lax
from jax.experimental import pallas as pl
from jax.experimental.pallas import tpu as pltpu
from jax.sharding import PartitionSpec as P

F32, BF16, I32 = jnp.float32, jnp.bfloat16, jnp.int32
MESH = pl.DeviceIdType.MESH
NZ, NP = 8, 32
ROWS, HALF, FR, C = 256, 128, 8, 128
NB = 8
GROUPS = NP // NB
BINS = 64
SLOTS = 2 * NZ * NP


def elu(x):
    low = jnp.exp(x) - 1.0
    return jnp.maximum(x.astype(BF16), jnp.minimum(low.astype(BF16), 0.0))


def dot(a, b):
    return jnp.dot(a, b, preferred_element_type=F32)


def dot_nt(a, b):
    return lax.dot_general(a, b, (((1,), (1,)), ((), ())), preferred_element_type=F32)


def iota(shape, axis):
    return lax.broadcasted_iota(I32, shape, axis)


def hot(mask):
    return jnp.where(mask, 1.0, 0.0).astype(BF16)


def lanes(parts):
    return jnp.concatenate(parts, axis=1)


def bytes_of(ref, sem):
    return pltpu.make_async_copy(ref, ref, sem)


def residual(skip, act, wd, wp, rows, stack):
    def body(step, carry):
        bases = [6 * (step * stack + n) for n in range(stack)]
        taps = jnp.concatenate(
            [
                lanes(
                    [act[pl.ds(t + 3 * i, 3), rows].reshape(3 * HALF, C) for i in range(4)]
                )
                for t in bases
            ],
            axis=0,
        )
        outer = dot(elu(dot(taps, wd[...])), wp[...])
        for n, t in enumerate(bases):
            for i in range(2):
                piece = outer[n * 3 * HALF : (n + 1) * 3 * HALF, C * i : C * (i + 1)]
                at = pl.ds(t + 3 * i, 3)
                old = skip[at, rows].astype(F32)
                skip[at, rows] = (old + piece.reshape(3, HALF, C)).astype(BF16)
        return carry

    return body


def kernel(
    g, w1_in, w2_in, w2d_in, w2p_in, w3_in, w3d_in, w3p_in, w4_in, cb_in, codes_in, dest, bins,
    out_code, out_latent, out_fold,
    w1, w2, w2d, w2p, w3, w3d, w3p, w4, cb, codes,
    w1_wide, w2d_pair, w2p_pair, w3d_pair, w3p_pair,
    got, s_mid, s_act, t_mid, t_act, order, place, relay, lat,
    meta_tab, meta_z, meta_mid, meta_own, tab, rows_z, rows_mid, rows_own, meta_t, count, dec, x,
    load_sem, own_sem, g_send, g_recv, mz_send, mz_recv, mp_send, mp_recv,
    z_send, z_recv, p_send, p_recv,
):
    z, p = lax.axis_index("shot"), lax.axis_index("trace")

    loads = [
        pltpu.make_async_copy(src, dst, load_sem.at[i])
        for i, (src, dst) in enumerate(
            [
                (codes_in, codes), (w1_in, w1), (w2_in, w2), (w2d_in, w2d), (w2p_in, w2p),
                (w3_in, w3), (w3d_in, w3d), (w3p_in, w3p), (w4_in, w4), (cb_in, cb),
            ]
        )
    ]
    for load in loads:
        load.start()
    own_block = pltpu.make_async_copy(
        g.at[:, :, pl.ds(pl.multiple_of(p * C, C), C)], got.at[p], own_sem
    )
    own_block.start()

    barrier = pltpu.get_barrier_semaphore()

    def greet_plane(j, carry):
        pl.semaphore_signal(
            barrier, inc=1, device_id={"trace": lax.rem(p + j, NP)}, device_id_type=MESH
        )
        return carry

    def greet_z(j, carry):
        pl.semaphore_signal(
            barrier, inc=1, device_id={"shot": lax.rem(z + j, NZ)}, device_id_type=MESH
        )
        return carry

    lax.fori_loop(1, NP, greet_plane, 0)
    lax.fori_loop(1, NZ, greet_z, 0)
    pl.semaphore_wait(barrier, NP - 1 + NZ - 1)

    def send_block(j, carry):
        to = lax.rem(p - j + NP, NP)
        pltpu.make_async_remote_copy(
            src_ref=g.at[:, :, pl.ds(pl.multiple_of(to * C, C), C)],
            dst_ref=got.at[p],
            send_sem=g_send,
            recv_sem=g_recv.at[j // NB],
            device_id={"trace": to},
            device_id_type=MESH,
        ).start()
        return carry

    lax.fori_loop(1, NP, send_block, 0)

    sub, lane = iota((ROWS, ROWS), 0), iota((ROWS, ROWS), 1)
    dest_row = dest[...]
    dest_f = dest_row.astype(F32)
    dest_col = jnp.sum(jnp.where(sub == lane, dest_f, 0.0), axis=1, keepdims=True)
    same = dest_col == dest_f
    rank_row = jnp.sum(jnp.where(same & (sub < lane), 1.0, 0.0), axis=0, keepdims=True)
    rank_col = jnp.sum(jnp.where(same & (lane < sub), 1.0, 0.0), axis=1, keepdims=True)
    seconds_before = jnp.sum(
        jnp.where((rank_col > 0.5) & (sub < lane), 1.0, 0.0), axis=0, keepdims=True
    )
    seconds = jnp.sum(rank_row, axis=1, keepdims=True)
    index = iota((1, ROWS), 1).astype(F32)
    position = jnp.where(rank_row > 0.5, seconds_before, seconds + index - seconds_before)
    order[...] = hot(position == sub.astype(F32))
    owner_hit = dest_row == sub
    slot_hot = [hot(owner_hit & (rank_row < 0.5)), hot(owner_hit & (rank_row > 0.5))]
    for r in range(2):
        place[r] = dot_nt(slot_hot[r], order[...]).astype(BF16)
    i, j = iota((SLOTS, SLOTS), 0), iota((SLOTS, SLOTS), 1)
    relay[...] = hot(j == (i % 16) * 32 + i // 16)

    loads[0].wait()
    ids = lanes([codes[s].reshape(64, HALF) for s in range(2)])
    low, high = ids & 255, ids >> 8
    marks = jnp.where(iota((C, ROWS), 0) == 0, bins[...] + 1, 0)
    meta = jnp.concatenate(
        [part.astype(F32).astype(BF16) for part in (low, high, marks)], axis=0
    )
    for r in range(2):
        meta_tab[:, r] = dot_nt(slot_hot[r], meta).astype(BF16).reshape(NZ, NP, 2 * C)
    meta_z[z] = meta_tab[z]

    def send_meta_z(j, carry):
        to = lax.rem(z + j, NZ)
        pltpu.make_async_remote_copy(
            src_ref=meta_tab.at[to],
            dst_ref=meta_z.at[z],
            send_sem=mz_send,
            recv_sem=mz_recv,
            device_id={"shot": to},
            device_id_type=MESH,
        ).start()
        return carry

    lax.fori_loop(1, NZ, send_meta_z, 0)

    for load in loads[1:9]:
        load.wait()
    tall = jnp.concatenate([w1[...].astype(F32)] * 32, axis=0)
    for t in range(16):
        w1_wide[:, C * t : C * (t + 1)] = jnp.where(iota((C, C), 0) % 64 // 4 == t, tall, 0.0).astype(
            BF16
        )
    zero = jnp.zeros((C, C), BF16)
    for wd, wp, wd_pair, wp_pair in ((w2d, w2p, w2d_pair, w2p_pair), (w3d, w3p, w3d_pair, w3p_pair)):
        wd_pair[0 : 3 * C, 0:C] = wd[...]
        wd_pair[3 * C : 4 * C, 0:C] = zero
        wd_pair[0:C, C : 2 * C] = zero
        wd_pair[C : 4 * C, C : 2 * C] = wd[...]
        wp_pair[0:C, 0:C] = wp[...]
        wp_pair[0:C, C : 2 * C] = zero
        wp_pair[C : 2 * C, 0:C] = zero
        wp_pair[C : 2 * C, C : 2 * C] = wp[...]
    edge = jnp.zeros((ROWS, C), BF16)
    for act, frames in ((s_act, 128), (t_act, 32)):
        for n in range(3):
            act[n] = edge
        for n in range(act.shape[0] - frames - 3):
            act[frames + 3 + n] = edge
    for mid, frames in ((s_mid, 128), (t_mid, 32)):
        for n in range(mid.shape[0] - frames):
            mid[frames + n] = edge

    own_block.wait()
    bytes_of(got.at[pl.ds(0, NB - 1)], g_recv.at[0]).wait()

    def send_meta_p(j, carry):
        to = lax.rem(p + j, NP)
        pltpu.make_async_remote_copy(
            src_ref=meta_mid.at[to],
            dst_ref=meta_own.at[p],
            send_sem=mp_send,
            recv_sem=mp_recv,
            device_id={"trace": to},
            device_id_type=MESH,
        ).start()
        return carry

    def encode_group(i, carry):
        @pl.when(i > 0)
        def _():
            bytes_of(got.at[pl.ds(0, NB)], g_recv.at[i]).wait()

        @pl.when(i == 2)
        def _():
            bytes_of(meta_z.at[pl.ds(0, NZ - 1)], mz_recv).wait()
            moved = dot(relay[...], meta_z[...].reshape(SLOTS, 2 * C)).astype(BF16)
            meta_mid[...] = moved.reshape(NP, 16, 2 * C)
            meta_own[p] = meta_mid[p]
            lax.fori_loop(1, NP, send_meta_p, 0)

        sources = [lax.rem(p + i * NB + n, NP) for n in range(NB)]
        samples = jnp.concatenate([lanes([got[s, 0], got[s, 1]]) for s in sources], axis=0)
        sorted_rows = dot_nt(order[...], samples).astype(BF16)
        for n in range(NB):
            pair = sorted_rows[:, C * (n // 2) : C * (n // 2 + 1)]
            mine = iota((ROWS, C), 1) // 64 == n % 2
            x[n * ROWS : (n + 1) * ROWS] = jnp.where(mine, pair, jnp.zeros_like(pair))

        def quarter(q, carry):
            at = pl.ds(pl.multiple_of(4 * C * q, 4 * C), 4 * C)
            first = elu(dot(x[...], w1_wide[:, at]))
            second = elu(dot(first, w2[...]))
            active = elu(second.astype(F32))
            for n, s in enumerate(sources):
                part = slice(n * ROWS, (n + 1) * ROWS)
                s_mid[4 * s + q] = second[part]
                s_act[4 * s + q + 3] = active[part]
            return carry

        lax.fori_loop(0, 4, quarter, 0)
        return carry

    lax.fori_loop(0, GROUPS, encode_group, 0)

    def send_z(r, c):
        def go(j, carry):
            to = lax.rem(z + j, NZ)
            pltpu.make_async_remote_copy(
                src_ref=tab.at[r, to, pl.ds(2 * c, 2)],
                dst_ref=rows_z.at[z, r, pl.ds(2 * c, 2)],
                send_sem=z_send.at[c],
                recv_sem=z_recv.at[c],
                device_id={"shot": to},
                device_id_type=MESH,
            ).start()
            return carry

        lax.fori_loop(1, NZ, go, 0)

    lat[...] = jnp.zeros_like(lat)

    def encode_half(h, carry):
        rows = pl.ds(pl.multiple_of(h * HALF, HALF), HALF)
        lax.fori_loop(0, 2, residual(s_mid, s_act, w2d_pair, w2p_pair, rows, 11), 0)

        def third(j, carry):
            taps = jnp.concatenate(
                [
                    lanes([s_mid[4 * (16 * j + n) + i, rows] for i in range(4)])
                    for n in range(16)
                ],
                axis=0,
            )
            u = elu(dot(taps, w3[...]))
            active = elu(u.astype(F32))
            t_mid[pl.ds(16 * j, 16), rows] = u.reshape(16, HALF, C)
            t_act[pl.ds(16 * j + 3, 16), rows] = active.reshape(16, HALF, C)
            return carry

        lax.fori_loop(0, 2, third, 0)
        residual(t_mid, t_act, w3d_pair, w3p_pair, rows, 6)(0, 0)
        taps = jnp.concatenate(
            [lanes([t_mid[4 * n + i, rows] for i in range(4)]) for n in range(8)], axis=0
        )
        lat[:, rows] = dot(taps, w4[...]).astype(BF16).reshape(FR, HALF, C)

        r = 1 - h

        def ship(c, carry):
            wide = lanes([lat[2 * c], lat[2 * c + 1]])
            table = dot(place[r], wide).astype(BF16)
            for n in range(2):
                tab[r, :, 2 * c + n] = table[:, C * n : C * (n + 1)].reshape(NZ, NP, C)
            rows_z[z, r, pl.ds(2 * c, 2)] = tab[r, z, pl.ds(2 * c, 2)]
            send_z(r, c)
            return carry

        lax.fori_loop(0, 4, ship, 0)
        return carry

    lax.fori_loop(0, 2, encode_half, 0)

    bytes_of(meta_own.at[pl.ds(0, NP - 1)], mp_recv).wait()
    loads[9].wait()

    meta_t[...] = dot_nt(
        hot(iota((2 * C, 2 * C), 0) == iota((2 * C, 2 * C), 1)),
        meta_own[...].reshape(SLOTS, 2 * C),
    )
    bin_row = meta_t[C : C + 1]
    sub = iota((4 * BINS, SLOTS), 0).astype(F32).astype(BF16)

    def count_codes(f, carry):
        a, b = iota((2 * C, C), 0), iota((2 * C, C), 1)
        picked = dot(meta_own[...].reshape(SLOTS, 2 * C), hot((a == 8 * f + b) & (b < 8))).astype(BF16)
        rows = pl.ds(pl.multiple_of(BINS * f, BINS), BINS)
        wide = iota((SLOTS, 4 * BINS), 1).astype(F32).astype(BF16)
        one, nil = jnp.ones((), BF16), jnp.zeros((), BF16)
        for k in range(8):
            group = meta_t[pl.ds(64 + 8 * f + k, 1)] * BINS + bin_row - 1.0
            low = picked[:, k : k + 1] == wide
            found = dot(
                jnp.where(group.astype(BF16) == sub, one, nil), jnp.where(low, one, nil)
            ).astype(BF16)
            for n in range(4):
                count[k, rows, 256 * n : 256 * (n + 1)] = found[BINS * n : BINS * (n + 1)]
        return carry

    def relay_rows(c, carry):
        lax.fori_loop(2 * c, 2 * c + 2, count_codes, 0)
        bytes_of(rows_z.at[pl.ds(0, NZ - 1), :, pl.ds(2 * c, 2)], z_recv.at[c]).wait()
        both = lanes([rows_z[:, :, 2 * c + n].reshape(SLOTS, C) for n in range(2)])
        moved = dot(relay[...], both).astype(BF16)
        for n in range(2):
            rows_mid[:, 2 * c + n] = moved[:, C * n : C * (n + 1)].reshape(NP, 16, C)
        rows_own[p, pl.ds(2 * c, 2)] = rows_mid[p, pl.ds(2 * c, 2)]

        def send_p(j, carry):
            to = lax.rem(p + j, NP)
            pltpu.make_async_remote_copy(
                src_ref=rows_mid.at[to, pl.ds(2 * c, 2)],
                dst_ref=rows_own.at[p, pl.ds(2 * c, 2)],
                send_sem=p_send.at[c],
                recv_sem=p_recv.at[c],
                device_id={"trace": to},
                device_id_type=MESH,
            ).start()
            return carry

        lax.fori_loop(1, NP, send_p, 0)
        return carry

    lax.fori_loop(0, 4, relay_rows, 0)

    dec[...] = jnp.zeros_like(dec)

    def decode(k, carry):
        dec[...] += dot(count[k], cb[k])
        return carry

    lax.fori_loop(0, 8, decode, 0)
    is_member = bin_row == (iota((BINS, SLOTS), 0) + 1).astype(F32)
    fold = jnp.maximum(jnp.sum(jnp.where(is_member, 1.0, 0.0), axis=1, keepdims=True), 1.0)
    out_fold[...] = jnp.broadcast_to(fold, (BINS, C))
    member = hot(is_member)
    for f in range(FR):
        out_code[:, f, :] = dec[BINS * f : BINS * (f + 1)]
    for c in range(4):
        f0 = 2 * c
        bytes_of(rows_own.at[pl.ds(0, NP - 1), pl.ds(f0, 2)], p_recv.at[c]).wait()
        both = lanes([rows_own[:, f0 + n].reshape(SLOTS, C) for n in range(2)])
        sums = dot(member, both)
        for n in range(2):
            out_latent[:, f0 + n, :] = sums[:, C * n : C * (n + 1)]

    bytes_of(got.at[pl.ds(0, NP - 1)], g_send).wait()
    bytes_of(meta_z.at[pl.ds(0, NZ - 1)], mz_send).wait()
    bytes_of(meta_own.at[pl.ds(0, NP - 1)], mp_send).wait()
    for c in range(4):
        bytes_of(rows_z.at[pl.ds(0, NZ - 1), :, pl.ds(2 * c, 2)], z_send.at[c]).wait()
        bytes_of(rows_own.at[pl.ds(0, NP - 1), pl.ds(2 * c, 2)], p_send.at[c]).wait()


def on_device(
    gathers, w1, w2, w2d, w2p, w3, w3d, w3p, w4, codebooks, codes, dest, bins
):
    hbm, vmem = pl.BlockSpec(memory_space=pl.ANY), pl.BlockSpec(memory_space=pltpu.VMEM)
    scratch = [
        ((4, C), BF16), ((4 * C, C), BF16), ((3 * C, C), BF16), ((C, C), BF16),
        ((4 * C, C), BF16), ((3 * C, C), BF16), ((C, C), BF16), ((4 * C, C), BF16),
        ((8, 1024, C), BF16), ((2, 8, 8, HALF), I32),
        ((C, 16 * C), BF16), ((4 * C, 2 * C), BF16), ((2 * C, 2 * C), BF16),
        ((4 * C, 2 * C), BF16), ((2 * C, 2 * C), BF16),
        ((NP, 2, 64, C), BF16),
        ((132, ROWS, C), BF16), ((138, ROWS, C), BF16),
        ((36, ROWS, C), BF16), ((42, ROWS, C), BF16),
        ((ROWS, ROWS), BF16), ((2, ROWS, ROWS), BF16), ((SLOTS, SLOTS), BF16),
        ((FR, ROWS, C), BF16),
        ((NZ, 2, NP, 2 * C), BF16), ((NZ, 2, NP, 2 * C), BF16),
        ((NP, 16, 2 * C), BF16), ((NP, 16, 2 * C), BF16),
        ((2, NZ, FR, NP, C), BF16), ((NZ, 2, FR, NP, C), BF16),
        ((NP, FR, 16, C), BF16), ((NP, FR, 16, C), BF16),
        ((2 * C, SLOTS), F32), ((8, FR * BINS, 1024), BF16), ((FR * BINS, C), F32),
        ((NB * ROWS, C), BF16),
    ]
    dma = pltpu.SemaphoreType.DMA
    code_sum, latent_sum, fold = pl.pallas_call(
        kernel,
        out_shape=[jax.ShapeDtypeStruct((BINS, FR, C), F32)] * 2
        + [jax.ShapeDtypeStruct((BINS, C), F32)],
        in_specs=[hbm] * 11 + [vmem] * 2,
        out_specs=[vmem] * 3,
        scratch_shapes=[pltpu.VMEM(shape, kind) for shape, kind in scratch]
        + [
            dma((10,)), dma, dma, dma((GROUPS,)), dma, dma, dma, dma,
            dma((4,)), dma((4,)), dma((4,)), dma((4,)),
        ],
        compiler_params=pltpu.CompilerParams(
            collective_id=0, has_side_effects=True, vmem_limit_bytes=60 * 2**20
        ),
        name="codec_stack",
    )(
        gathers, w1, w2, w2d, w2p, w3, w3d, w3p, w4, codebooks,
        codes.transpose(0, 2, 3, 1), dest.reshape(1, ROWS), bins.reshape(1, ROWS),
    )
    fold = fold[:, None, :]
    return code_sum / fold, (latent_sum - code_sum) / fold


def solution(mesh):
    rows4, rows3 = P("shot", "trace", None, None), P("shot", "trace", None)
    out = P(("shot", "trace"), None, None)
    return jax.shard_map(
        on_device,
        mesh=mesh,
        in_specs=(rows3,) + (P(),) * 9 + (rows4, rows4, rows3),
        out_specs=(out, out),
        check_vma=False,
    )
```

```python
import jax
import jax.numpy as jnp
from jax import lax
from jax.experimental import pallas as pl
from jax.experimental.pallas import tpu as pltpu
from jax.sharding import PartitionSpec as P

F32, BF16, I32 = jnp.float32, jnp.bfloat16, jnp.int32
MESH = pl.DeviceIdType.MESH
NZ, NP = 8, 32
ROWS, HALF, FR, C = 256, 128, 8, 128
NB = 8
GROUPS = NP // NB
STRIDE = 13
BINS = 64
SLOTS = 2 * NZ * NP


def elu(x):
    low = jnp.exp(x) - 1.0
    return jnp.maximum(x.astype(BF16), jnp.minimum(low.astype(BF16), 0.0))


def dot(a, b):
    return jnp.dot(a, b, preferred_element_type=F32)


def dot_nt(a, b):
    return lax.dot_general(a, b, (((1,), (1,)), ((), ())), preferred_element_type=F32)


def iota(shape, axis):
    return lax.broadcasted_iota(I32, shape, axis)


def hot(mask):
    return jnp.where(mask, 1.0, 0.0).astype(BF16)


def lanes(parts):
    return jnp.concatenate(parts, axis=1)


def bytes_of(ref, sem):
    return pltpu.make_async_copy(ref, ref, sem)


def residual(skip, act, wd, wp, rows, stack):
    def body(step, carry):
        bases = [6 * (step * stack + n) for n in range(stack)]
        taps = jnp.concatenate(
            [
                lanes(
                    [act[pl.ds(t + 3 * i, 3), rows].reshape(3 * HALF, C) for i in range(4)]
                )
                for t in bases
            ],
            axis=0,
        )
        outer = dot(elu(dot(taps, wd[...])), wp[...])
        for n, t in enumerate(bases):
            for i in range(2):
                piece = outer[n * 3 * HALF : (n + 1) * 3 * HALF, C * i : C * (i + 1)]
                at = pl.ds(t + 3 * i, 3)
                old = skip[at, rows].astype(F32)
                skip[at, rows] = (old + piece.reshape(3, HALF, C)).astype(BF16)
        return carry

    return body


def kernel(
    g, w1_in, w2_in, w2d_in, w2p_in, w3_in, w3d_in, w3p_in, w4_in, cb_in, codes_in, dest, bins,
    out_code, out_latent, out_fold,
    w1, w2, w2d, w2p, w3, w3d, w3p, w4, cb, codes,
    w1_wide, w2d_pair, w2p_pair, w3d_pair, w3p_pair,
    got, s_mid, s_act, t_mid, t_act, order, place, relay, lat,
    meta_tab, meta_z, meta_mid, meta_own, tab, rows_z, rows_mid, rows_own, meta_t, count, dec, x,
    load_sem, own_sem, g_send, g_recv, mz_send, mz_recv, mp_send, mp_recv,
    z_send, z_recv, p_send, p_recv,
):
    z, p = lax.axis_index("shot"), lax.axis_index("trace")

    loads = [
        pltpu.make_async_copy(src, dst, load_sem.at[i])
        for i, (src, dst) in enumerate(
            [
                (codes_in, codes), (w1_in, w1), (w2_in, w2), (w2d_in, w2d), (w2p_in, w2p),
                (w3_in, w3), (w3d_in, w3d), (w3p_in, w3p), (w4_in, w4), (cb_in, cb),
            ]
        )
    ]
    for load in loads:
        load.start()
    own_block = pltpu.make_async_copy(
        g.at[:, :, pl.ds(pl.multiple_of(p * C, C), C)], got.at[p], own_sem
    )
    own_block.start()

    barrier = pltpu.get_barrier_semaphore()

    def greet_plane(j, carry):
        pl.semaphore_signal(
            barrier, inc=1, device_id={"trace": lax.rem(p + j, NP)}, device_id_type=MESH
        )
        return carry

    def greet_z(j, carry):
        pl.semaphore_signal(
            barrier, inc=1, device_id={"shot": lax.rem(z + j, NZ)}, device_id_type=MESH
        )
        return carry

    lax.fori_loop(1, NP, greet_plane, 0)
    lax.fori_loop(1, NZ, greet_z, 0)
    pl.semaphore_wait(barrier, NP - 1 + NZ - 1)

    def send_block(j, carry):
        to = lax.rem(p + (NP - STRIDE) * j, NP)
        pltpu.make_async_remote_copy(
            src_ref=g.at[:, :, pl.ds(pl.multiple_of(to * C, C), C)],
            dst_ref=got.at[p],
            send_sem=g_send,
            recv_sem=g_recv.at[j // NB],
            device_id={"trace": to},
            device_id_type=MESH,
        ).start()
        return carry

    lax.fori_loop(1, NP, send_block, 0)

    sub, lane = iota((ROWS, ROWS), 0), iota((ROWS, ROWS), 1)
    dest_row = dest[...]
    dest_f = dest_row.astype(F32)
    dest_col = jnp.sum(jnp.where(sub == lane, dest_f, 0.0), axis=1, keepdims=True)
    same = dest_col == dest_f
    rank_row = jnp.sum(jnp.where(same & (sub < lane), 1.0, 0.0), axis=0, keepdims=True)
    rank_col = jnp.sum(jnp.where(same & (lane < sub), 1.0, 0.0), axis=1, keepdims=True)
    seconds_before = jnp.sum(
        jnp.where((rank_col > 0.5) & (sub < lane), 1.0, 0.0), axis=0, keepdims=True
    )
    seconds = jnp.sum(rank_row, axis=1, keepdims=True)
    index = iota((1, ROWS), 1).astype(F32)
    position = jnp.where(rank_row > 0.5, seconds_before, seconds + index - seconds_before)
    order[...] = hot(position == sub.astype(F32))
    owner_hit = dest_row == sub
    slot_hot = [hot(owner_hit & (rank_row < 0.5)), hot(owner_hit & (rank_row > 0.5))]
    for r in range(2):
        place[r] = dot_nt(slot_hot[r], order[...]).astype(BF16)
    i, j = iota((SLOTS, SLOTS), 0), iota((SLOTS, SLOTS), 1)
    relay[...] = hot(j == (i % 16) * 32 + i // 16)

    loads[0].wait()
    ids = lanes([codes[s].reshape(64, HALF) for s in range(2)])
    low, high = ids & 255, ids >> 8
    marks = jnp.where(iota((C, ROWS), 0) == 0, bins[...] + 1, 0)
    meta = jnp.concatenate(
        [part.astype(F32).astype(BF16) for part in (low, high, marks)], axis=0
    )
    for r in range(2):
        meta_tab[:, r] = dot_nt(slot_hot[r], meta).astype(BF16).reshape(NZ, NP, 2 * C)
    meta_z[z] = meta_tab[z]

    def send_meta_z(j, carry):
        to = lax.rem(z + 3 * j, NZ)
        pltpu.make_async_remote_copy(
            src_ref=meta_tab.at[to],
            dst_ref=meta_z.at[z],
            send_sem=mz_send,
            recv_sem=mz_recv,
            device_id={"shot": to},
            device_id_type=MESH,
        ).start()
        return carry

    lax.fori_loop(1, NZ, send_meta_z, 0)

    for load in loads[1:9]:
        load.wait()
    tall = jnp.concatenate([w1[...].astype(F32)] * 32, axis=0)
    for t in range(16):
        w1_wide[:, C * t : C * (t + 1)] = jnp.where(iota((C, C), 0) % 64 // 4 == t, tall, 0.0).astype(
            BF16
        )
    zero = jnp.zeros((C, C), BF16)
    for wd, wp, wd_pair, wp_pair in ((w2d, w2p, w2d_pair, w2p_pair), (w3d, w3p, w3d_pair, w3p_pair)):
        wd_pair[0 : 3 * C, 0:C] = wd[...]
        wd_pair[3 * C : 4 * C, 0:C] = zero
        wd_pair[0:C, C : 2 * C] = zero
        wd_pair[C : 4 * C, C : 2 * C] = wd[...]
        wp_pair[0:C, 0:C] = wp[...]
        wp_pair[0:C, C : 2 * C] = zero
        wp_pair[C : 2 * C, 0:C] = zero
        wp_pair[C : 2 * C, C : 2 * C] = wp[...]
    edge = jnp.zeros((ROWS, C), BF16)
    for act, frames in ((s_act, 128), (t_act, 32)):
        for n in range(3):
            act[n] = edge
        for n in range(act.shape[0] - frames - 3):
            act[frames + 3 + n] = edge
    for mid, frames in ((s_mid, 128), (t_mid, 32)):
        for n in range(mid.shape[0] - frames):
            mid[frames + n] = edge

    own_block.wait()
    bytes_of(got.at[pl.ds(0, NB - 1)], g_recv.at[0]).wait()

    def send_meta_p(j, carry):
        to = lax.rem(p + STRIDE * j, NP)
        pltpu.make_async_remote_copy(
            src_ref=meta_mid.at[to],
            dst_ref=meta_own.at[p],
            send_sem=mp_send,
            recv_sem=mp_recv,
            device_id={"trace": to},
            device_id_type=MESH,
        ).start()
        return carry

    def encode_group(i, carry):
        @pl.when(i > 0)
        def _():
            bytes_of(got.at[pl.ds(0, NB)], g_recv.at[i]).wait()

        @pl.when(i == 2)
        def _():
            bytes_of(meta_z.at[pl.ds(0, NZ - 1)], mz_recv).wait()
            moved = dot(relay[...], meta_z[...].reshape(SLOTS, 2 * C)).astype(BF16)
            meta_mid[...] = moved.reshape(NP, 16, 2 * C)
            meta_own[p] = meta_mid[p]
            lax.fori_loop(1, NP, send_meta_p, 0)

        sources = [lax.rem(p + STRIDE * (i * NB + n), NP) for n in range(NB)]
        samples = jnp.concatenate([lanes([got[s, 0], got[s, 1]]) for s in sources], axis=0)
        sorted_rows = dot_nt(order[...], samples).astype(BF16)
        for n in range(NB):
            pair = sorted_rows[:, C * (n // 2) : C * (n // 2 + 1)]
            mine = iota((ROWS, C), 1) // 64 == n % 2
            x[n * ROWS : (n + 1) * ROWS] = jnp.where(mine, pair, jnp.zeros_like(pair))

        def quarter(q, carry):
            at = pl.ds(pl.multiple_of(4 * C * q, 4 * C), 4 * C)
            first = elu(dot(x[...], w1_wide[:, at]))
            second = elu(dot(first, w2[...]))
            active = elu(second.astype(F32))
            for n, s in enumerate(sources):
                part = slice(n * ROWS, (n + 1) * ROWS)
                s_mid[4 * s + q] = second[part]
                s_act[4 * s + q + 3] = active[part]
            return carry

        lax.fori_loop(0, 4, quarter, 0)
        return carry

    lax.fori_loop(0, GROUPS, encode_group, 0)

    def send_z(r, c):
        def go(j, carry):
            to = lax.rem(z + 3 * j, NZ)
            pltpu.make_async_remote_copy(
                src_ref=tab.at[r, to, pl.ds(2 * c, 2)],
                dst_ref=rows_z.at[z, r, pl.ds(2 * c, 2)],
                send_sem=z_send.at[c],
                recv_sem=z_recv.at[c],
                device_id={"shot": to},
                device_id_type=MESH,
            ).start()
            return carry

        lax.fori_loop(1, NZ, go, 0)

    lat[...] = jnp.zeros_like(lat)

    def encode_half(h, carry):
        rows = pl.ds(pl.multiple_of(h * HALF, HALF), HALF)
        lax.fori_loop(0, 2, residual(s_mid, s_act, w2d_pair, w2p_pair, rows, 11), 0)

        def third(j, carry):
            taps = jnp.concatenate(
                [
                    lanes([s_mid[4 * (16 * j + n) + i, rows] for i in range(4)])
                    for n in range(16)
                ],
                axis=0,
            )
            u = elu(dot(taps, w3[...]))
            active = elu(u.astype(F32))
            t_mid[pl.ds(16 * j, 16), rows] = u.reshape(16, HALF, C)
            t_act[pl.ds(16 * j + 3, 16), rows] = active.reshape(16, HALF, C)
            return carry

        lax.fori_loop(0, 2, third, 0)
        residual(t_mid, t_act, w3d_pair, w3p_pair, rows, 6)(0, 0)
        taps = jnp.concatenate(
            [lanes([t_mid[4 * n + i, rows] for i in range(4)]) for n in range(8)], axis=0
        )
        lat[:, rows] = dot(taps, w4[...]).astype(BF16).reshape(FR, HALF, C)

        r = 1 - h

        def ship(c, carry):
            wide = lanes([lat[2 * c], lat[2 * c + 1]])
            table = dot(place[r], wide).astype(BF16)
            for n in range(2):
                tab[r, :, 2 * c + n] = table[:, C * n : C * (n + 1)].reshape(NZ, NP, C)
            rows_z[z, r, pl.ds(2 * c, 2)] = tab[r, z, pl.ds(2 * c, 2)]
            send_z(r, c)
            return carry

        lax.fori_loop(0, 4, ship, 0)
        return carry

    lax.fori_loop(0, 2, encode_half, 0)

    bytes_of(meta_own.at[pl.ds(0, NP - 1)], mp_recv).wait()
    loads[9].wait()

    meta_t[...] = dot_nt(
        hot(iota((2 * C, 2 * C), 0) == iota((2 * C, 2 * C), 1)),
        meta_own[...].reshape(SLOTS, 2 * C),
    )
    bin_row = meta_t[C : C + 1]
    sub = iota((4 * BINS, SLOTS), 0).astype(F32).astype(BF16)

    def count_codes(f, carry):
        a, b = iota((2 * C, C), 0), iota((2 * C, C), 1)
        picked = dot(meta_own[...].reshape(SLOTS, 2 * C), hot((a == 8 * f + b) & (b < 8))).astype(BF16)
        rows = pl.ds(pl.multiple_of(BINS * f, BINS), BINS)
        wide = iota((SLOTS, 4 * BINS), 1).astype(F32).astype(BF16)
        one, nil = jnp.ones((), BF16), jnp.zeros((), BF16)
        for k in range(8):
            group = meta_t[pl.ds(64 + 8 * f + k, 1)] * BINS + bin_row - 1.0
            low = picked[:, k : k + 1] == wide
            found = dot(
                jnp.where(group.astype(BF16) == sub, one, nil), jnp.where(low, one, nil)
            ).astype(BF16)
            for n in range(4):
                count[k, rows, 256 * n : 256 * (n + 1)] = found[BINS * n : BINS * (n + 1)]
        return carry

    def relay_rows(c, carry):
        lax.fori_loop(2 * c, 2 * c + 2, count_codes, 0)
        bytes_of(rows_z.at[pl.ds(0, NZ - 1), :, pl.ds(2 * c, 2)], z_recv.at[c]).wait()
        both = lanes([rows_z[:, :, 2 * c + n].reshape(SLOTS, C) for n in range(2)])
        moved = dot(relay[...], both).astype(BF16)
        for n in range(2):
            rows_mid[:, 2 * c + n] = moved[:, C * n : C * (n + 1)].reshape(NP, 16, C)
        rows_own[p, pl.ds(2 * c, 2)] = rows_mid[p, pl.ds(2 * c, 2)]

        def send_p(j, carry):
            to = lax.rem(p + STRIDE * j, NP)
            pltpu.make_async_remote_copy(
                src_ref=rows_mid.at[to, pl.ds(2 * c, 2)],
                dst_ref=rows_own.at[p, pl.ds(2 * c, 2)],
                send_sem=p_send.at[c],
                recv_sem=p_recv.at[c],
                device_id={"trace": to},
                device_id_type=MESH,
            ).start()
            return carry

        lax.fori_loop(1, NP, send_p, 0)
        return carry

    lax.fori_loop(0, 4, relay_rows, 0)

    dec[...] = jnp.zeros_like(dec)

    def decode(k, carry):
        dec[...] += dot(count[k], cb[k])
        return carry

    lax.fori_loop(0, 8, decode, 0)
    is_member = bin_row == (iota((BINS, SLOTS), 0) + 1).astype(F32)
    fold = jnp.maximum(jnp.sum(jnp.where(is_member, 1.0, 0.0), axis=1, keepdims=True), 1.0)
    out_fold[...] = jnp.broadcast_to(fold, (BINS, C))
    member = hot(is_member)
    for f in range(FR):
        out_code[:, f, :] = dec[BINS * f : BINS * (f + 1)]
    for c in range(4):
        f0 = 2 * c
        bytes_of(rows_own.at[pl.ds(0, NP - 1), pl.ds(f0, 2)], p_recv.at[c]).wait()
        both = lanes([rows_own[:, f0 + n].reshape(SLOTS, C) for n in range(2)])
        sums = dot(member, both)
        for n in range(2):
            out_latent[:, f0 + n, :] = sums[:, C * n : C * (n + 1)]

    bytes_of(got.at[pl.ds(0, NP - 1)], g_send).wait()
    bytes_of(meta_z.at[pl.ds(0, NZ - 1)], mz_send).wait()
    bytes_of(meta_own.at[pl.ds(0, NP - 1)], mp_send).wait()
    for c in range(4):
        bytes_of(rows_z.at[pl.ds(0, NZ - 1), :, pl.ds(2 * c, 2)], z_send.at[c]).wait()
        bytes_of(rows_own.at[pl.ds(0, NP - 1), pl.ds(2 * c, 2)], p_send.at[c]).wait()


def on_device(
    gathers, w1, w2, w2d, w2p, w3, w3d, w3p, w4, codebooks, codes, dest, bins
):
    hbm, vmem = pl.BlockSpec(memory_space=pl.ANY), pl.BlockSpec(memory_space=pltpu.VMEM)
    scratch = [
        ((4, C), BF16), ((4 * C, C), BF16), ((3 * C, C), BF16), ((C, C), BF16),
        ((4 * C, C), BF16), ((3 * C, C), BF16), ((C, C), BF16), ((4 * C, C), BF16),
        ((8, 1024, C), BF16), ((2, 8, 8, HALF), I32),
        ((C, 16 * C), BF16), ((4 * C, 2 * C), BF16), ((2 * C, 2 * C), BF16),
        ((4 * C, 2 * C), BF16), ((2 * C, 2 * C), BF16),
        ((NP, 2, 64, C), BF16),
        ((132, ROWS, C), BF16), ((138, ROWS, C), BF16),
        ((36, ROWS, C), BF16), ((42, ROWS, C), BF16),
        ((ROWS, ROWS), BF16), ((2, ROWS, ROWS), BF16), ((SLOTS, SLOTS), BF16),
        ((FR, ROWS, C), BF16),
        ((NZ, 2, NP, 2 * C), BF16), ((NZ, 2, NP, 2 * C), BF16),
        ((NP, 16, 2 * C), BF16), ((NP, 16, 2 * C), BF16),
        ((2, NZ, FR, NP, C), BF16), ((NZ, 2, FR, NP, C), BF16),
        ((NP, FR, 16, C), BF16), ((NP, FR, 16, C), BF16),
        ((2 * C, SLOTS), F32), ((8, FR * BINS, 1024), BF16), ((FR * BINS, C), F32),
        ((NB * ROWS, C), BF16),
    ]
    dma = pltpu.SemaphoreType.DMA
    code_sum, latent_sum, fold = pl.pallas_call(
        kernel,
        out_shape=[jax.ShapeDtypeStruct((BINS, FR, C), F32)] * 2
        + [jax.ShapeDtypeStruct((BINS, C), F32)],
        in_specs=[hbm] * 11 + [vmem] * 2,
        out_specs=[vmem] * 3,
        scratch_shapes=[pltpu.VMEM(shape, kind) for shape, kind in scratch]
        + [
            dma((10,)), dma, dma, dma((GROUPS,)), dma, dma, dma, dma,
            dma((4,)), dma((4,)), dma((4,)), dma((4,)),
        ],
        compiler_params=pltpu.CompilerParams(
            collective_id=0, has_side_effects=True, vmem_limit_bytes=60 * 2**20
        ),
        name="codec_stack",
    )(
        gathers, w1, w2, w2d, w2p, w3, w3d, w3p, w4, codebooks,
        codes.transpose(0, 2, 3, 1), dest.reshape(1, ROWS), bins.reshape(1, ROWS),
    )
    fold = fold[:, None, :]
    return code_sum / fold, (latent_sum - code_sum) / fold


def solution(mesh):
    rows4, rows3 = P("shot", "trace", None, None), P("shot", "trace", None)
    out = P(("shot", "trace"), None, None)
    return jax.shard_map(
        on_device,
        mesh=mesh,
        in_specs=(rows3,) + (P(),) * 9 + (rows4, rows4, rows3),
        out_specs=(out, out),
        check_vma=False,
    )
```

```python
import jax
import jax.numpy as jnp
from jax import lax
from jax.experimental import pallas as pl
from jax.experimental.pallas import tpu as pltpu
from jax.sharding import PartitionSpec as P

F32, BF16, I32 = jnp.float32, jnp.bfloat16, jnp.int32
MESH = pl.DeviceIdType.MESH
NZ, NP = 8, 32
ROWS, PART, FR, C = 256, 64, 8, 128
NB = 8
GROUPS = NP // NB
STRIDE = 13
BINS = 64
SLOTS = 2 * NZ * NP


def elu(x):
    low = jnp.exp(x) - 1.0
    return jnp.maximum(x.astype(BF16), jnp.minimum(low.astype(BF16), 0.0))


def dot(a, b):
    return jnp.dot(a, b, preferred_element_type=F32)


def dot_nt(a, b):
    return lax.dot_general(a, b, (((1,), (1,)), ((), ())), preferred_element_type=F32)


def iota(shape, axis):
    return lax.broadcasted_iota(I32, shape, axis)


def hot(mask):
    return jnp.where(mask, 1.0, 0.0).astype(BF16)


def lanes(parts):
    return jnp.concatenate(parts, axis=1)


def bytes_of(ref, sem):
    return pltpu.make_async_copy(ref, ref, sem)


def residual(skip, act, wd, wp, rows, stack):
    def body(step, carry):
        bases = [6 * (step * stack + n) for n in range(stack)]
        taps = jnp.concatenate(
            [
                lanes(
                    [act[pl.ds(t + 3 * i, 3), rows].reshape(3 * PART, C) for i in range(4)]
                )
                for t in bases
            ],
            axis=0,
        )
        outer = dot(elu(dot(taps, wd[...])), wp[...])
        for n, t in enumerate(bases):
            for i in range(2):
                piece = outer[n * 3 * PART : (n + 1) * 3 * PART, C * i : C * (i + 1)]
                at = pl.ds(t + 3 * i, 3)
                old = skip[at, rows].astype(F32)
                skip[at, rows] = (old + piece.reshape(3, PART, C)).astype(BF16)
        return carry

    return body


def kernel(
    g, w1_in, w2_in, w2d_in, w2p_in, w3_in, w3d_in, w3p_in, w4_in, cb_in, codes_in, dest, bins,
    out_code, out_latent, out_fold,
    w1, w2, w2d, w2p, w3, w3d, w3p, w4, cb, codes,
    w1_wide, w2d_pair, w2p_pair, w3d_pair, w3p_pair,
    got, s_mid, s_act, t_mid, t_act, order, place, relay, lat,
    meta_tab, meta_z, meta_mid, meta_own, tab, rows_z, rows_mid, rows_own, meta_t, count, dec, x,
    load_sem, own_sem, g_send, g_recv, mz_send, mz_recv, mp_send, mp_recv,
    z_send, z_recv, p_send, p_recv,
):
    z, p = lax.axis_index("shot"), lax.axis_index("trace")

    loads = [
        pltpu.make_async_copy(src, dst, load_sem.at[i])
        for i, (src, dst) in enumerate(
            [
                (codes_in, codes), (w1_in, w1), (w2_in, w2), (w2d_in, w2d), (w2p_in, w2p),
                (w3_in, w3), (w3d_in, w3d), (w3p_in, w3p), (w4_in, w4), (cb_in, cb),
            ]
        )
    ]
    for load in loads:
        load.start()
    own_block = pltpu.make_async_copy(
        g.at[:, :, pl.ds(pl.multiple_of(p * C, C), C)], got.at[p], own_sem
    )
    own_block.start()

    barrier = pltpu.get_barrier_semaphore()

    def greet_plane(j, carry):
        pl.semaphore_signal(
            barrier, inc=1, device_id={"trace": lax.rem(p + j, NP)}, device_id_type=MESH
        )
        return carry

    def greet_z(j, carry):
        pl.semaphore_signal(
            barrier, inc=1, device_id={"shot": lax.rem(z + j, NZ)}, device_id_type=MESH
        )
        return carry

    lax.fori_loop(1, NP, greet_plane, 0)
    lax.fori_loop(1, NZ, greet_z, 0)
    pl.semaphore_wait(barrier, NP - 1 + NZ - 1)

    def send_block(j, carry):
        to = lax.rem(p + (NP - STRIDE) * j, NP)
        pltpu.make_async_remote_copy(
            src_ref=g.at[:, :, pl.ds(pl.multiple_of(to * C, C), C)],
            dst_ref=got.at[p],
            send_sem=g_send,
            recv_sem=g_recv.at[j // NB],
            device_id={"trace": to},
            device_id_type=MESH,
        ).start()
        return carry

    lax.fori_loop(1, NP, send_block, 0)

    sub, lane = iota((ROWS, ROWS), 0), iota((ROWS, ROWS), 1)
    dest_row = dest[...]
    dest_f = dest_row.astype(F32)
    dest_col = jnp.sum(jnp.where(sub == lane, dest_f, 0.0), axis=1, keepdims=True)
    same = dest_col == dest_f
    rank_row = jnp.sum(jnp.where(same & (sub < lane), 1.0, 0.0), axis=0, keepdims=True)
    rank_col = jnp.sum(jnp.where(same & (lane < sub), 1.0, 0.0), axis=1, keepdims=True)
    seconds_before = jnp.sum(
        jnp.where((rank_col > 0.5) & (sub < lane), 1.0, 0.0), axis=0, keepdims=True
    )
    seconds = jnp.sum(rank_row, axis=1, keepdims=True)
    away = ((dest_row + (ROWS - NP * lax.rem(z + 4, NZ))) & (ROWS - 1)).astype(F32)
    away_col = jnp.sum(jnp.where(sub == lane, away, 0.0), axis=1, keepdims=True)
    firsts_before = jnp.sum(
        jnp.where((rank_col < 0.5) & (away_col < away), 1.0, 0.0), axis=0, keepdims=True
    )
    position = jnp.where(rank_row > 0.5, seconds_before, seconds + firsts_before)
    order[...] = hot(position == sub.astype(F32))
    owner_hit = dest_row == sub
    slot_hot = [hot(owner_hit & (rank_row < 0.5)), hot(owner_hit & (rank_row > 0.5))]
    for r in range(2):
        place[r] = dot_nt(slot_hot[r], order[...]).astype(BF16)
    i, j = iota((SLOTS, SLOTS), 0), iota((SLOTS, SLOTS), 1)
    relay[...] = hot(j == (i % 16) * 32 + i // 16)

    loads[0].wait()
    ids = lanes([codes[s].reshape(64, C) for s in range(2)])
    low, high = ids & 255, ids >> 8
    marks = jnp.where(iota((C, ROWS), 0) == 0, bins[...] + 1, 0)
    meta = jnp.concatenate(
        [part.astype(F32).astype(BF16) for part in (low, high, marks)], axis=0
    )
    for r in range(2):
        meta_tab[:, r] = dot_nt(slot_hot[r], meta).astype(BF16).reshape(NZ, NP, 2 * C)
    meta_z[z] = meta_tab[z]

    def send_meta_z(j, carry):
        to = lax.rem(z + 3 * j, NZ)
        pltpu.make_async_remote_copy(
            src_ref=meta_tab.at[to],
            dst_ref=meta_z.at[z],
            send_sem=mz_send,
            recv_sem=mz_recv,
            device_id={"shot": to},
            device_id_type=MESH,
        ).start()
        return carry

    lax.fori_loop(1, NZ, send_meta_z, 0)

    for load in loads[1:9]:
        load.wait()
    tall = jnp.concatenate([w1[...].astype(F32)] * 32, axis=0)
    for t in range(16):
        w1_wide[:, C * t : C * (t + 1)] = jnp.where(iota((C, C), 0) % 64 // 4 == t, tall, 0.0).astype(
            BF16
        )
    zero = jnp.zeros((C, C), BF16)
    for wd, wp, wd_pair, wp_pair in ((w2d, w2p, w2d_pair, w2p_pair), (w3d, w3p, w3d_pair, w3p_pair)):
        wd_pair[0 : 3 * C, 0:C] = wd[...]
        wd_pair[3 * C : 4 * C, 0:C] = zero
        wd_pair[0:C, C : 2 * C] = zero
        wd_pair[C : 4 * C, C : 2 * C] = wd[...]
        wp_pair[0:C, 0:C] = wp[...]
        wp_pair[0:C, C : 2 * C] = zero
        wp_pair[C : 2 * C, 0:C] = zero
        wp_pair[C : 2 * C, C : 2 * C] = wp[...]
    edge = jnp.zeros((ROWS, C), BF16)
    for act, frames in ((s_act, 128), (t_act, 32)):
        for n in range(3):
            act[n] = edge
        for n in range(act.shape[0] - frames - 3):
            act[frames + 3 + n] = edge
    for mid, frames in ((s_mid, 128), (t_mid, 32)):
        for n in range(mid.shape[0] - frames):
            mid[frames + n] = edge

    own_block.wait()
    bytes_of(got.at[pl.ds(0, NB - 1)], g_recv.at[0]).wait()

    def send_meta_p(j, carry):
        to = lax.rem(p + STRIDE * j, NP)
        pltpu.make_async_remote_copy(
            src_ref=meta_mid.at[to],
            dst_ref=meta_own.at[p],
            send_sem=mp_send,
            recv_sem=mp_recv,
            device_id={"trace": to},
            device_id_type=MESH,
        ).start()
        return carry

    def encode_group(i, carry):
        @pl.when(i > 0)
        def _():
            bytes_of(got.at[pl.ds(0, NB)], g_recv.at[i]).wait()

        @pl.when(i == 2)
        def _():
            bytes_of(meta_z.at[pl.ds(0, NZ - 1)], mz_recv).wait()
            moved = dot(relay[...], meta_z[...].reshape(SLOTS, 2 * C)).astype(BF16)
            meta_mid[...] = moved.reshape(NP, 16, 2 * C)
            meta_own[p] = meta_mid[p]
            lax.fori_loop(1, NP, send_meta_p, 0)

        sources = [lax.rem(p + STRIDE * (i * NB + n), NP) for n in range(NB)]
        samples = jnp.concatenate([lanes([got[s, 0], got[s, 1]]) for s in sources], axis=0)
        sorted_rows = dot_nt(order[...], samples).astype(BF16)
        for n in range(NB):
            pair = sorted_rows[:, C * (n // 2) : C * (n // 2 + 1)]
            mine = iota((ROWS, C), 1) // 64 == n % 2
            x[n * ROWS : (n + 1) * ROWS] = jnp.where(mine, pair, jnp.zeros_like(pair))

        def quarter(q, carry):
            at = pl.ds(pl.multiple_of(4 * C * q, 4 * C), 4 * C)
            first = elu(dot(x[...], w1_wide[:, at]))
            second = elu(dot(first, w2[...]))
            active = elu(second.astype(F32))
            for n, s in enumerate(sources):
                part = slice(n * ROWS, (n + 1) * ROWS)
                s_mid[4 * s + q] = second[part]
                s_act[4 * s + q + 3] = active[part]
            return carry

        lax.fori_loop(0, 4, quarter, 0)
        return carry

    lax.fori_loop(0, GROUPS, encode_group, 0)

    def send_z(r, slot, c, offsets):
        for offset in offsets:
            to = lax.rem(z + offset, NZ)
            pltpu.make_async_remote_copy(
                src_ref=tab.at[slot, to, pl.ds(2 * c, 2)],
                dst_ref=rows_z.at[z, r, pl.ds(2 * c, 2)],
                send_sem=z_send.at[c],
                recv_sem=z_recv.at[c],
                device_id={"shot": to},
                device_id_type=MESH,
            ).start()

    lat[...] = jnp.zeros_like(lat)

    def encode_part(h, carry):
        rows = pl.ds(pl.multiple_of(h * PART, PART), PART)
        lax.fori_loop(0, 1, residual(s_mid, s_act, w2d_pair, w2p_pair, rows, 22), 0)

        def third(j, carry):
            taps = jnp.concatenate(
                [
                    lanes([s_mid[4 * (32 * j + n) + i, rows] for i in range(4)])
                    for n in range(32)
                ],
                axis=0,
            )
            u = elu(dot(taps, w3[...]))
            active = elu(u.astype(F32))
            t_mid[pl.ds(32 * j, 32), rows] = u.reshape(32, PART, C)
            t_act[pl.ds(32 * j + 3, 32), rows] = active.reshape(32, PART, C)
            return carry

        third(0, 0)
        residual(t_mid, t_act, w3d_pair, w3p_pair, rows, 6)(0, 0)
        taps = jnp.concatenate(
            [lanes([t_mid[4 * n + i, rows] for i in range(4)]) for n in range(8)], axis=0
        )
        lat[:, rows] = dot(taps, w4[...]).astype(BF16).reshape(FR, PART, C)

        for part, r, slot, offsets in (
            (1, 1, 1, (4, 3, 5, 2, 6, 1, 7)), (2, 0, 2, (4, 5)), (3, 0, 0, (3, 6, 2, 7, 1))
        ):

            @pl.when(h == part)
            def _(r=r, slot=slot, offsets=offsets):
                def ship(c, carry):
                    wide = lanes([lat[2 * c], lat[2 * c + 1]])
                    table = dot(place[r], wide).astype(BF16)
                    for n in range(2):
                        tab[slot, :, 2 * c + n] = table[:, C * n : C * (n + 1)].reshape(NZ, NP, C)
                    rows_z[z, r, pl.ds(2 * c, 2)] = tab[slot, z, pl.ds(2 * c, 2)]
                    send_z(r, slot, c, offsets)
                    return carry

                lax.fori_loop(0, 4, ship, 0)

        return carry

    lax.fori_loop(0, 4, encode_part, 0)

    bytes_of(meta_own.at[pl.ds(0, NP - 1)], mp_recv).wait()
    loads[9].wait()

    meta_t[...] = dot_nt(
        hot(iota((2 * C, 2 * C), 0) == iota((2 * C, 2 * C), 1)),
        meta_own[...].reshape(SLOTS, 2 * C),
    )
    bin_row = meta_t[C : C + 1]
    sub = iota((4 * BINS, SLOTS), 0).astype(F32).astype(BF16)

    def count_codes(f, carry):
        a, b = iota((2 * C, C), 0), iota((2 * C, C), 1)
        picked = dot(meta_own[...].reshape(SLOTS, 2 * C), hot((a == 8 * f + b) & (b < 8))).astype(BF16)
        rows = pl.ds(pl.multiple_of(BINS * f, BINS), BINS)
        wide = iota((SLOTS, 4 * BINS), 1).astype(F32).astype(BF16)
        one, nil = jnp.ones((), BF16), jnp.zeros((), BF16)
        for k in range(8):
            group = meta_t[pl.ds(64 + 8 * f + k, 1)] * BINS + bin_row - 1.0
            low = picked[:, k : k + 1] == wide
            found = dot(
                jnp.where(group.astype(BF16) == sub, one, nil), jnp.where(low, one, nil)
            ).astype(BF16)
            for n in range(4):
                count[k, rows, 256 * n : 256 * (n + 1)] = found[BINS * n : BINS * (n + 1)]
        return carry

    def relay_rows(c, carry):
        lax.fori_loop(2 * c, 2 * c + 2, count_codes, 0)
        bytes_of(rows_z.at[pl.ds(0, NZ - 1), :, pl.ds(2 * c, 2)], z_recv.at[c]).wait()
        both = lanes([rows_z[:, :, 2 * c + n].reshape(SLOTS, C) for n in range(2)])
        moved = dot(relay[...], both).astype(BF16)
        for n in range(2):
            rows_mid[:, 2 * c + n] = moved[:, C * n : C * (n + 1)].reshape(NP, 16, C)
        rows_own[p, pl.ds(2 * c, 2)] = rows_mid[p, pl.ds(2 * c, 2)]

        def send_p(j, carry):
            to = lax.rem(p + STRIDE * j, NP)
            pltpu.make_async_remote_copy(
                src_ref=rows_mid.at[to, pl.ds(2 * c, 2)],
                dst_ref=rows_own.at[p, pl.ds(2 * c, 2)],
                send_sem=p_send.at[c],
                recv_sem=p_recv.at[c],
                device_id={"trace": to},
                device_id_type=MESH,
            ).start()
            return carry

        lax.fori_loop(1, NP, send_p, 0)
        return carry

    lax.fori_loop(0, 4, relay_rows, 0)

    dec[...] = jnp.zeros_like(dec)

    def decode(k, carry):
        dec[...] += dot(count[k], cb[k])
        return carry

    lax.fori_loop(0, 8, decode, 0)
    is_member = bin_row == (iota((BINS, SLOTS), 0) + 1).astype(F32)
    fold = jnp.maximum(jnp.sum(jnp.where(is_member, 1.0, 0.0), axis=1, keepdims=True), 1.0)
    out_fold[...] = jnp.broadcast_to(fold, (BINS, C))
    member = hot(is_member)
    for f in range(FR):
        out_code[:, f, :] = dec[BINS * f : BINS * (f + 1)]
    for c in range(4):
        f0 = 2 * c
        bytes_of(rows_own.at[pl.ds(0, NP - 1), pl.ds(f0, 2)], p_recv.at[c]).wait()
        both = lanes([rows_own[:, f0 + n].reshape(SLOTS, C) for n in range(2)])
        sums = dot(member, both)
        for n in range(2):
            out_latent[:, f0 + n, :] = sums[:, C * n : C * (n + 1)]

    bytes_of(got.at[pl.ds(0, NP - 1)], g_send).wait()
    bytes_of(meta_z.at[pl.ds(0, NZ - 1)], mz_send).wait()
    bytes_of(meta_own.at[pl.ds(0, NP - 1)], mp_send).wait()
    for c in range(4):
        bytes_of(rows_z.at[pl.ds(0, NZ - 1), :, pl.ds(2 * c, 2)], z_send.at[c]).wait()
        bytes_of(rows_own.at[pl.ds(0, NP - 1), pl.ds(2 * c, 2)], p_send.at[c]).wait()


def on_device(
    gathers, w1, w2, w2d, w2p, w3, w3d, w3p, w4, codebooks, codes, dest, bins
):
    hbm, vmem = pl.BlockSpec(memory_space=pl.ANY), pl.BlockSpec(memory_space=pltpu.VMEM)
    scratch = [
        ((4, C), BF16), ((4 * C, C), BF16), ((3 * C, C), BF16), ((C, C), BF16),
        ((4 * C, C), BF16), ((3 * C, C), BF16), ((C, C), BF16), ((4 * C, C), BF16),
        ((8, 1024, C), BF16), ((2, 8, 8, C), I32),
        ((C, 16 * C), BF16), ((4 * C, 2 * C), BF16), ((2 * C, 2 * C), BF16),
        ((4 * C, 2 * C), BF16), ((2 * C, 2 * C), BF16),
        ((NP, 2, 64, C), BF16),
        ((132, ROWS, C), BF16), ((138, ROWS, C), BF16),
        ((36, ROWS, C), BF16), ((42, ROWS, C), BF16),
        ((ROWS, ROWS), BF16), ((2, ROWS, ROWS), BF16), ((SLOTS, SLOTS), BF16),
        ((FR, ROWS, C), BF16),
        ((NZ, 2, NP, 2 * C), BF16), ((NZ, 2, NP, 2 * C), BF16),
        ((NP, 16, 2 * C), BF16), ((NP, 16, 2 * C), BF16),
        ((3, NZ, FR, NP, C), BF16), ((NZ, 2, FR, NP, C), BF16),
        ((NP, FR, 16, C), BF16), ((NP, FR, 16, C), BF16),
        ((2 * C, SLOTS), F32), ((8, FR * BINS, 1024), BF16), ((FR * BINS, C), F32),
        ((NB * ROWS, C), BF16),
    ]
    dma = pltpu.SemaphoreType.DMA
    code_sum, latent_sum, fold = pl.pallas_call(
        kernel,
        out_shape=[jax.ShapeDtypeStruct((BINS, FR, C), F32)] * 2
        + [jax.ShapeDtypeStruct((BINS, C), F32)],
        in_specs=[hbm] * 11 + [vmem] * 2,
        out_specs=[vmem] * 3,
        scratch_shapes=[pltpu.VMEM(shape, kind) for shape, kind in scratch]
        + [
            dma((10,)), dma, dma, dma((GROUPS,)), dma, dma, dma, dma,
            dma((4,)), dma((4,)), dma((4,)), dma((4,)),
        ],
        compiler_params=pltpu.CompilerParams(
            collective_id=0, has_side_effects=True, vmem_limit_bytes=60 * 2**20
        ),
        name="codec_stack",
    )(
        gathers, w1, w2, w2d, w2p, w3, w3d, w3p, w4, codebooks,
        codes.transpose(0, 2, 3, 1), dest.reshape(1, ROWS), bins.reshape(1, ROWS),
    )
    fold = fold[:, None, :]
    return code_sum / fold, (latent_sum - code_sum) / fold


def solution(mesh):
    rows4, rows3 = P("shot", "trace", None, None), P("shot", "trace", None)
    out = P(("shot", "trace"), None, None)
    return jax.shard_map(
        on_device,
        mesh=mesh,
        in_specs=(rows3,) + (P(),) * 9 + (rows4, rows4, rows3),
        out_specs=(out, out),
        check_vma=False,
    )
```
